256 devices in a mesh: exp: 128 (over x, z, y), dp: 2 (over core).
Axes of the slice: x: 4, y: 4, z: 8, core: 2. Of those that a mesh axis runs over, the one named last changes fastest.
Arguments:
- grad_out: bfloat16 [32768, 2880], P(('exp', 'dp')), may hold values from -6 to 6
- combine: float32 [32768, 4], P(('exp', 'dp')), may hold values from 0.05 to 0.6
- routes: int32 [32768, 4], P(('exp', 'dp')), may hold values from 0 to 127, as said below
- tasks: int32 [32768], P(('exp', 'dp')), may hold values from 0 to 3, as said below
- task_lists: int32 [4, 64], replicated, may hold values from 0 to 127, as said below
- gate_up: bfloat16 [128, 1536, 2880], P('exp', 'dp'), may hold values from -6 to 6
Outputs:
- grad_down: bfloat16 [128, 1440, 2880], P('exp', 'dp')
The draws below stay inside these ranges and needn't reach their ends.
Inputs may be any that keep to these rules, and one draw needn't show every extreme that they name: `routes`: in the 128 tokens of one device no expert is named more than 6 times, and some expert is named exactly 6 times; each token names 4 different experts. `tasks`: all 128 tokens of one device belong to one task. `task_lists`: each row names 64 different experts.
All inputs are finite; a program needn't handle non-finite values.
Results may differ from the reference program's by a relative error of at most 0.0057.
Values may be sent and summed in bfloat16 or wider, within the bound.
A program may use at most 128 MiB of HBM per device.

```python
import jax
import jax.numpy as jnp
from jax import lax

D = 2880
FF = 1440
TOP = 4
TASKS = 4
TOK_DEV = 128
EXPERTS = 128
TOKENS = 32768
CAP = 6
ROWS_DEV = 768
ROWS_EXP = 1536
LIST = 64
N_DP = 2


def joint_draw(key):
    list_key, task_key, drop_key, extra_key, order_key, token_key = jax.random.split(key, 6)
    task_keys = jax.random.split(list_key, TASKS)
    lists = jax.vmap(lambda one_key: jax.random.permutation(one_key, EXPERTS)[:LIST])(task_keys).astype(jnp.int32)
    blocks = TOKENS // TOK_DEV
    block_task = jax.random.randint(task_key, (blocks,), 0, TASKS).astype(jnp.int32)
    expert_ids = jnp.arange(EXPERTS, dtype=jnp.int32)
    member_table = jnp.any(lists[:, :, None] == expert_ids[None, None, :], axis=1)
    member = member_table[block_task]
    first_listed = lists[block_task, 0]
    drops = jax.random.randint(drop_key, (blocks, EXPERTS), 0, CAP // 3 + 1).astype(jnp.int32)
    drops = jnp.where(expert_ids[None, :] == first_listed[:, None], 0, drops)
    listed_quota = CAP - drops
    listed_sum = jnp.sum(jnp.where(member, listed_quota, 0), axis=1)
    remain = TOK_DEV * TOP - listed_sum
    others = EXPERTS - LIST
    base_count = remain // others
    extra_count = remain % others
    scores = jax.random.randint(extra_key, (blocks, EXPERTS), 0, 1 << 20).astype(jnp.int32) * EXPERTS + expert_ids[None, :]
    scores = scores + member.astype(jnp.int32) * (EXPERTS * (1 << 20))
    ranked = jnp.argsort(jnp.argsort(scores, axis=1), axis=1)
    quota = jnp.where(member, listed_quota, base_count[:, None] + (ranked < extra_count[:, None]).astype(jnp.int32))
    order_scores = jax.random.randint(order_key, (blocks, EXPERTS), 0, 1 << 20).astype(jnp.int32) * EXPERTS + expert_ids[None, :]
    expert_order = jnp.argsort(order_scores, axis=1).astype(jnp.int32)
    ordered_quota = jnp.take_along_axis(quota, expert_order, axis=1)
    ends = jnp.cumsum(ordered_quota, axis=1)
    positions = jnp.arange(TOK_DEV * TOP, dtype=jnp.int32)
    which = jax.vmap(lambda edge: jnp.searchsorted(edge, positions, side='right'))(ends).astype(jnp.int32)
    sequence = jnp.take_along_axis(expert_order, which, axis=1)
    routes_block = jnp.transpose(sequence.reshape(blocks, TOP, TOK_DEV), (0, 2, 1))
    token_scores = jax.random.randint(token_key, (blocks, TOK_DEV), 0, 1 << 20).astype(jnp.int32) * TOK_DEV + jnp.arange(TOK_DEV, dtype=jnp.int32)[None, :]
    token_order = jnp.argsort(token_scores, axis=1).astype(jnp.int32)
    routes = jnp.take_along_axis(routes_block, token_order[:, :, None], axis=1).reshape(TOKENS, TOP)
    tasks = jnp.repeat(block_task, TOK_DEV)
    return (lists, tasks.astype(jnp.int32), routes.astype(jnp.int32))


def draw_task_lists(key, part):
    lists, tasks, routes = joint_draw(key)
    return lists


def draw_tasks(key, part):
    lists, tasks, routes = joint_draw(key)
    return tasks


def draw_routes(key, part):
    lists, tasks, routes = joint_draw(key)
    return routes


def levels(stream_key, dims, cuts, smallest, top_value):
    factor_of, own = 1.0, jax.random.fold_in(stream_key, 6)
    for dim, parts in cuts:
        steps = jnp.exp(jax.random.uniform(jax.random.fold_in(own, dim), (parts,), jnp.float32, smallest / len(cuts), top_value / len(cuts)))
        factor_of = factor_of * jnp.repeat(steps, dims[dim] // parts).reshape([-1 if axis == dim else 1 for axis in range(len(dims))])
    return factor_of


def scatter_about(rng, shape, scale, most, pieces=(), kind=jnp.bfloat16):
    array = jax.random.normal(rng, shape, jnp.float32) * scale
    if len(pieces) > 0:
        array = levels(rng, shape, pieces, -0.22, 0.18) * array
    return jnp.clip(array, min=-most, max=most).astype(kind)


def setup_inputs(seed: int = 0) -> dict:
    keys = jax.random.split(jax.random.key(seed), 7)
    return {
        "grad_out": scatter_about(keys[0], (TOKENS, D), 1.0, 6.0, ((0, 256),)),
        "combine": jnp.clip(0.05 + 0.55 * jax.random.uniform(keys[1], (TOKENS, TOP), jnp.float32) ** levels(keys[1], (TOKENS, TOP), ((0, 256),), -0.2, 0.2), 0.05, 0.6),
        "routes": draw_routes(jax.random.fold_in(keys[6], 71), 0),
        "tasks": draw_tasks(jax.random.fold_in(keys[6], 71), 0),
        "task_lists": draw_task_lists(jax.random.fold_in(keys[6], 71), 0),
        "gate_up": scatter_about(keys[5], (EXPERTS, ROWS_EXP, 2 * FF), 1.0, 6.0, ((0, 128), (1, 2))),
    }


def expert_hidden(gate_up):
    half_width = gate_up.shape[-1] // 2
    gate_pre = gate_up[..., :half_width].astype(jnp.float32)
    up_pre = gate_up[..., half_width:].astype(jnp.float32)
    return ((up_pre + 1.0) * gate_pre * jax.nn.sigmoid(1.702 * gate_pre)).astype(jnp.bfloat16)


def reference(grad_out, combine, routes, tasks, task_lists, gate_up):
    expert_ids = jnp.arange(EXPERTS, dtype=jnp.int32)
    member = jnp.any(task_lists[:, :, None] == expert_ids[None, None, :], axis=1)
    keep_flags = member[tasks[:, None], routes]
    onehot = (routes.reshape(TOKENS // TOK_DEV, TOK_DEV * TOP, 1) == expert_ids[None, None, :]).astype(jnp.int32)
    running = jnp.cumsum(onehot, axis=1) - 1
    slot_index = jnp.sum(onehot * running, axis=2).reshape(-1)
    block_index = jnp.arange(TOKENS * TOP, dtype=jnp.int32) // (TOK_DEV * TOP)
    source = block_index // N_DP
    part_index = block_index % N_DP
    destination = routes.reshape(-1) * ROWS_EXP + part_index * ROWS_DEV + source * CAP + slot_index
    source_of_slot = jnp.full((EXPERTS * ROWS_EXP,), -1, jnp.int32).at[destination].set(
        jnp.arange(TOKENS * TOP, dtype=jnp.int32))
    keep_flat = keep_flags.reshape(-1)
    weight_flat = combine.reshape(-1)

    def one_expert(expert):
        picked = lax.dynamic_slice_in_dim(source_of_slot, (expert * ROWS_EXP).astype(jnp.int32), ROWS_EXP)
        is_valid = picked >= 0
        safe_index = jnp.maximum(picked, 0)
        routed_rows = (weight_flat[safe_index][:, None] * grad_out[safe_index // TOP].astype(jnp.float32)).astype(jnp.bfloat16)
        is_live = is_valid & keep_flat[safe_index]
        masked = jnp.where(is_live[:, None], routed_rows, jnp.zeros_like(routed_rows))
        hidden = expert_hidden(gate_up[expert])
        total = lax.dot_general(hidden, masked, (((0,), (0,)), ((), ())), preferred_element_type=jnp.float32)
        return total.astype(jnp.bfloat16)

    return lax.map(one_expert, expert_ids)
```

```python
import functools

import jax
import jax.numpy as jnp
from jax import lax
from jax.experimental import pallas as pl
from jax.experimental.pallas import tpu as pltpu
from jax.sharding import PartitionSpec as P

F32, BF16, I32 = jnp.float32, jnp.bfloat16, jnp.int32
MESH = pl.DeviceIdType.MESH
GRID = {128: (4, 8, 4), 8: (2, 2, 2)}
CAPACITY = {128: 80, 8: 16}
CHUNK = {2880: 512, 320: 128}


def expert_hidden(gate_up):
    half_width = gate_up.shape[-1] // 2
    gate_pre = gate_up[..., :half_width].astype(jnp.float32)
    up_pre = gate_up[..., half_width:].astype(jnp.float32)
    return ((up_pre + 1.0) * gate_pre * jax.nn.sigmoid(1.702 * gate_pre)).astype(jnp.bfloat16)


def outer_rows(left_rows, right_rows):
    return lax.dot_general(
        left_rows, right_rows, (((0,), (0,)), ((), ())), preferred_element_type=jnp.float32
    )


def dense_body(grad_out, combine, routes, tasks, task_lists, gate_up):
    n_experts = lax.axis_size("exp")
    slot_rows = gate_up.shape[1]
    capacity = slot_rows // n_experts
    model_width = grad_out.shape[1]
    tok_count = routes.shape[0]
    top_count = routes.shape[1]
    task_count = task_lists.shape[0]
    expert_ids = lax.iota(jnp.int32, n_experts)
    member = jnp.any(task_lists[:, :, None] == expert_ids[None, None, :], axis=1).astype(
        jnp.float32
    )
    task_onehot = (tasks[:, None] == lax.iota(jnp.int32, task_count)[None, :]).astype(jnp.float32)
    token_member = jnp.dot(task_onehot, member) > 0.5
    route_onehot = (routes[:, :, None] == expert_ids[None, None, :]).astype(jnp.int32)
    keep_flags = jnp.sum(route_onehot * token_member[:, None, :].astype(jnp.int32), axis=2)
    flat_onehot = route_onehot.reshape(tok_count * top_count, n_experts)
    running = jnp.cumsum(flat_onehot, axis=0) - 1
    slot_index = jnp.sum(flat_onehot * running, axis=1)
    destination = routes.reshape(-1) * capacity + slot_index
    routed = (combine[:, :, None] * grad_out[:, None, :].astype(jnp.float32)).astype(jnp.bfloat16)
    routed = routed.reshape(tok_count * top_count, model_width)
    send_rows = (
        jnp.zeros((n_experts * capacity, model_width), jnp.bfloat16).at[destination].set(routed)
    )
    send_keep = (
        jnp.zeros((n_experts * capacity,), jnp.bfloat16)
        .at[destination]
        .set(keep_flags.reshape(-1).astype(jnp.bfloat16))
    )
    recv_rows, recv_keep = (
        lax.all_to_all(send_rows, "exp", split_axis=0, concat_axis=0, tiled=True),
        lax.all_to_all(send_keep, "exp", split_axis=0, concat_axis=0, tiled=True),
    )
    masked = jnp.where(recv_keep[:, None] > 0, recv_rows, jnp.zeros_like(recv_rows))
    hidden = expert_hidden(gate_up[0])
    summed = lax.psum_scatter(outer_rows(hidden, masked), "dp", scatter_dimension=0, tiled=True)
    return summed.astype(jnp.bfloat16)


def iota(shape, dim):
    return lax.broadcasted_iota(I32, shape, dim)


def whole_part(values, step):
    return jnp.floor((values.astype(F32) + 0.5) * (1.0 / step)).astype(I32)


def dot(left, right):
    return jnp.dot(left, right, preferred_element_type=F32)


def dot_lanes(left, right):
    return lax.dot_general(left, right, (((1,), (1,)), ((), ())), preferred_element_type=F32)


def tiles_of(width, step):
    return [(start, min(step, width - start)) for start in range(0, width, step)]


def kernel(
    sizes, tok_ref, comb_ref, routes_ref, task_ref, lists_ref, gate_up_ref,
    out_ref, flag_ref, *scratch,
):
    (nx, nz, ny), cap, cap_rows, room, chunks = sizes
    n_chunks = len(chunks)
    width, tok_count = tok_ref.shape
    double, slot_rows = gate_up_ref.shape
    hidden_width = double // 2
    half = hidden_width // 2
    experts, plane = nx * nz * ny, nx * ny
    block = nz * cap

    scratch = list(scratch)
    take = lambda count: [scratch.pop(0) for _ in range(count)]
    z_send, z_recv, xy_send, xy_recv = (take(n_chunks) for _ in range(4))
    own, dp_send, dp_recv, out_buf = (take(n_chunks) for _ in range(4))
    pick, gu, hidden, spread, weight = take(5)
    meta_send, meta_recv, note_send, note_recv, last_send, last_recv = take(6)
    zs_sem, zr_sem, xs_sem, xr_sem, ds_sem, dr_sem, out_sem = take(7)
    ms_sem, mr_sem, ns_sem, nr_sem, ls_sem, lr_sem, gu_sem = take(7)
    zl_sem, xl_sem, ml_sem, nl_sem = take(4)

    e_id, p = lax.axis_index("exp"), lax.axis_index("dp")
    y = lax.rem(e_id, ny)
    z = lax.rem(lax.div(e_id, ny), nz)
    x = lax.div(e_id, ny * nz)
    q = x * ny + y
    z_steps = sorted(range(1, nz), key=lambda d: -min(d, nz - d))
    xy_steps = sorted(
        ((dx, dy) for dx in range(nx) for dy in range(ny) if dx or dy),
        key=lambda s: -(min(s[0], nx - s[0]) + min(s[1], ny - s[1])),
    )

    def z_at(z2):
        return ((x * nz + z2) * ny + y, p)

    def xy_at(x2, y2):
        return ((x2 * nz + z) * ny + y2, p)

    sibling = (e_id, 1 - p)

    gu_copy = pltpu.make_async_copy(gate_up_ref, gu, gu_sem)
    gu_copy.start()

    barrier = pltpu.get_barrier_semaphore()
    for d in z_steps:
        pl.semaphore_signal(barrier, inc=1, device_id=z_at(lax.rem(z + d, nz)), device_id_type=MESH)
    for dx, dy in xy_steps:
        pl.semaphore_signal(
            barrier, inc=1, device_id=xy_at(lax.rem(x + dx, nx), lax.rem(y + dy, ny)),
            device_id_type=MESH,
        )
    pl.semaphore_signal(barrier, inc=1, device_id=sibling, device_id_type=MESH)

    expert_col = iota((experts, tok_count), 0)
    named = jnp.zeros((experts, tok_count), F32)
    weight_of = jnp.zeros((experts, tok_count), F32)
    for k in range(routes_ref.shape[0]):
        hit = expert_col == routes_ref[k : k + 1, :]
        named = jnp.where(hit, 1.0, named)
        weight_of = jnp.where(hit, comb_ref[k : k + 1, :], weight_of)
    lists = lists_ref[...]
    of_task = iota(lists.shape, 0) == task_ref[0:1, 0:1]
    chosen = jnp.max(jnp.where(of_task, lists, -1), axis=0, keepdims=True)
    trainable = jnp.max(
        jnp.where(iota((experts, lists.shape[1]), 0) == chosen, 1.0, 0.0), axis=1, keepdims=True
    )
    before = jnp.where(
        iota((tok_count, tok_count), 0) < iota((tok_count, tok_count), 1), 1.0, 0.0
    ).astype(BF16)
    slot = dot(named.astype(BF16), before)
    live = named * trainable
    expert_plane = lax.rem(lax.shift_right_logical(iota((nz, experts), 1), ny.bit_length() - 1), nz)
    in_plane = jnp.where(expert_plane == iota((nz, experts), 0), 1.0, 0.0).astype(BF16)
    wanted = dot(in_plane, live.astype(BF16)) > 0.5
    place = dot(jnp.where(wanted, 1.0, 0.0).astype(BF16), before)
    over = jnp.max(jnp.where(wanted & (place > room - 0.5), 1.0, 0.0), axis=1, keepdims=True)
    over = jnp.max(over, axis=0, keepdims=True)
    place = jnp.where(wanted, place, -1.0)
    row_id = iota((room, tok_count), 0).astype(F32)
    for z2 in range(nz):
        pick[z2 * room : (z2 + 1) * room, :] = jnp.where(
            row_id == place[z2 : z2 + 1, :], 1.0, 0.0
        ).astype(BF16)

    def send_z(j):
        start, size = chunks[j]
        z_send[j][...] = (
            dot_lanes(pick[...], tok_ref[start : start + size, :])
            .astype(BF16)
            .reshape(z_send[j].shape)
        )
        for d in z_steps:
            z2 = lax.rem(z + d, nz)
            z_copy(j, z2).start()
        pltpu.make_async_copy(z_send[j].at[z], z_recv[j].at[z], zl_sem.at[j]).start()

    def z_copy(j, z2):
        return pltpu.make_async_remote_copy(
            src_ref=z_send[j].at[z2], dst_ref=z_recv[j].at[z],
            send_sem=zs_sem.at[j, z2], recv_sem=zr_sem.at[j, z],
            device_id=z_at(z2), device_id_type=MESH,
        )

    def meta_copy(z2):
        return pltpu.make_async_remote_copy(
            src_ref=meta_send, dst_ref=meta_recv.at[z],
            send_sem=ms_sem.at[z2], recv_sem=mr_sem.at[z],
            device_id=z_at(z2), device_id_type=MESH,
        )

    def wait_from(ref, sem, device):
        pltpu.make_async_remote_copy(
            src_ref=ref, dst_ref=ref, send_sem=sem, recv_sem=sem,
            device_id=device, device_id_type=MESH,
        ).wait_recv()

    pl.semaphore_wait(barrier, len(z_steps) + len(xy_steps) + 1)
    send_z(0)

    place_of = lax.dot_general(
        in_plane, place.astype(BF16), (((0,), (0,)), ((), ())), preferred_element_type=F32
    )
    meta_lane = iota((experts, 128), 1)
    meta = jnp.zeros((experts, 128), F32)
    for c in range(cap):
        here = jnp.where((slot > c - 0.5) & (slot < c + 0.5), live, 0.0)
        at = jnp.sum(here * (place_of + 1.0), axis=1, keepdims=True)
        w = jnp.sum(here * weight_of, axis=1, keepdims=True)
        high = w.astype(BF16).astype(F32)
        mid = (w - high).astype(BF16).astype(F32)
        for kind, value in enumerate((at, high, mid, w - high - mid)):
            meta = jnp.where(meta_lane == kind * cap_rows + c, value, meta)
    meta = jnp.where(meta_lane == cap, over, meta)
    meta_send[...] = jnp.transpose(meta)[: 4 * cap_rows, :].astype(BF16)
    for d in z_steps:
        meta_copy(lax.rem(z + d, nz)).start()
    pltpu.make_async_copy(meta_send, meta_recv.at[z], ml_sem).start()
    if n_chunks > 1:
        send_z(1)

    gu_copy.wait()
    step = 96 if hidden_width % 96 == 0 else 32

    @pl.loop(0, hidden_width // step)
    def _(i):
        rows = pl.ds(pl.multiple_of(i * step, step), step)
        gate = gu[rows, :].astype(F32)
        up = gu[pl.ds(pl.multiple_of(i * step + hidden_width, step), step), :].astype(F32)
        gu[rows, :] = ((up + 1.0) * gate * jax.nn.sigmoid(1.702 * gate)).astype(BF16)

    for start, size in tiles_of(slot_rows, 256):
        to = iota((slot_rows, size), 1) + start
        to_q = whole_part(to, block)
        rest = to - to_q * block
        to_z = whole_part(rest, cap)
        c = rest - to_z * cap
        to_x = whole_part(to_q, ny)
        source = ((to_x * nz + to_z) * ny + (to_q - to_x * ny)) * cap + c
        order = jnp.where(iota((slot_rows, size), 0) == source, 1.0, 0.0).astype(BF16)
        hidden[:, start : start + size] = dot(gu[0:hidden_width, :], order).astype(BF16)

    for d in z_steps:
        z2 = lax.rem(z + nz - d, nz)
        wait_from(meta_recv.at[z2], mr_sem.at[z2], z_at(z2))
    pltpu.make_async_copy(meta_send, meta_recv.at[z], ml_sem).wait()
    s_col = iota((slot_rows, experts), 0)
    s_q = whole_part(s_col, block)
    s_x = whole_part(s_q, ny)
    expert_of = (s_x * nz + z) * ny + (s_q - s_x * ny)
    at_expert = jnp.where(expert_of == iota((slot_rows, experts), 1), 1.0, 0.0).astype(BF16)
    m_col = iota((slot_rows, cap_rows * 4), 0)
    m_lane = iota((slot_rows, cap_rows * 4), 1)
    m_rest = m_col - whole_part(m_col, block) * block
    m_z = whole_part(m_rest, cap)
    m_c = m_rest - m_z * cap
    totals = jnp.zeros((slot_rows, cap_rows * 4), F32)
    noted = jnp.zeros((1, experts), F32)
    for z2 in range(nz):
        table = meta_recv[z2]
        noted = jnp.maximum(noted, table[cap : cap + 1, :].astype(F32))
        found = dot_lanes(at_expert, table)
        totals = jnp.where(m_z == z2, found, totals)
    kind_of = whole_part(m_lane, cap_rows)
    slot_hit = m_lane - kind_of * cap_rows == m_c
    at = jnp.sum(jnp.where(slot_hit & (kind_of == 0), totals, 0.0), axis=1, keepdims=True)
    w = jnp.sum(jnp.where(slot_hit & (kind_of > 0), totals, 0.0), axis=1, keepdims=True)
    weight[...] = jnp.broadcast_to(w, weight.shape)
    r_col = iota((slot_rows, 1), 0)
    r_rest = r_col - whole_part(r_col, block) * block
    at = jnp.where(at > 0.5, at - 1.0 + (whole_part(r_rest, cap) * room).astype(F32), -1.0)
    spread[...] = jnp.where(
        iota((slot_rows, nz * room), 1).astype(F32) == at, 1.0, 0.0
    ).astype(BF16)
    note_send[...] = jnp.broadcast_to(
        jnp.max(noted, axis=1, keepdims=True), note_send.shape
    ).astype(BF16)

    def note_copy(x2, y2):
        q2 = x2 * ny + y2
        return pltpu.make_async_remote_copy(
            src_ref=note_send, dst_ref=note_recv.at[q],
            send_sem=ns_sem.at[q2], recv_sem=nr_sem.at[q],
            device_id=xy_at(x2, y2), device_id_type=MESH,
        )

    def xy_copy(j, x2, y2):
        q2 = x2 * ny + y2
        return pltpu.make_async_remote_copy(
            src_ref=xy_send[j].at[q2], dst_ref=xy_recv[j].at[q],
            send_sem=xs_sem.at[j, q2], recv_sem=xr_sem.at[j, q],
            device_id=xy_at(x2, y2), device_id_type=MESH,
        )

    def dp_copy(j):
        return pltpu.make_async_remote_copy(
            src_ref=dp_send[j], dst_ref=dp_recv[j], send_sem=ds_sem.at[j], recv_sem=dr_sem.at[j],
            device_id=sibling, device_id_type=MESH,
        )

    def each_xy(act):
        for dx, dy in xy_steps:
            act(lax.rem(x + dx, nx), lax.rem(y + dy, ny))

    def send_xy(j):
        for d in z_steps:
            z2 = lax.rem(z + nz - d, nz)
            wait_from(z_recv[j].at[z2], zr_sem.at[j, z2], z_at(z2))
        pltpu.make_async_copy(z_send[j].at[z], z_recv[j].at[z], zl_sem.at[j]).wait()
        if j + 2 < n_chunks:
            send_z(j + 2)
        size = chunks[j][1]
        for start, part in tiles_of(size, 256):
            rows = z_recv[j][:, :, start : start + part].reshape(nz * room, part)
            found = dot(spread[...], rows)
            by = jnp.concatenate([weight[...]] * 2, axis=1)[:, :part]
            xy_send[j][:, :, start : start + part] = (found * by).astype(BF16).reshape(
                plane, block, part
            )
        each_xy(lambda x2, y2: xy_copy(j, x2, y2).start())
        pltpu.make_async_copy(xy_send[j].at[q], xy_recv[j].at[q], xl_sem.at[j]).start()

    def multiply(j):
        def arrived(x2, y2):
            q2 = x2 * ny + y2
            wait_from(xy_recv[j].at[q2], xr_sem.at[j, q2], xy_at(x2, y2))

        each_xy(arrived)
        pltpu.make_async_copy(xy_send[j].at[q], xy_recv[j].at[q], xl_sem.at[j]).wait()
        theirs = pl.ds(pl.multiple_of((1 - p) * half, 16), half)
        mine = pl.ds(pl.multiple_of(p * half, 16), half)
        size = chunks[j][1]
        for start, part in tiles_of(size, 256):
            rows = xy_recv[j][:, :, start : start + part].reshape(slot_rows, part)
            dp_send[j][:, start : start + part] = dot(hidden[theirs, :], rows).astype(BF16)
        dp_copy(j).start()
        for start, part in tiles_of(size, 256):
            rows = xy_recv[j][:, :, start : start + part].reshape(slot_rows, part)
            own[j][:, start : start + part] = dot(hidden[mine, :], rows)

    def out_copy(j):
        start, size = chunks[j]
        return pltpu.make_async_copy(
            out_buf[j], out_ref.at[:, start : start + size], out_sem.at[j]
        )

    def finish(j):
        dp_copy(j).wait_recv()
        out_buf[j][...] = (own[j][...] + dp_recv[j][...].astype(F32)).astype(BF16)
        out_copy(j).start()

    each_xy(lambda x2, y2: note_copy(x2, y2).start())
    pltpu.make_async_copy(note_send, note_recv.at[q], nl_sem).start()
    for j in range(n_chunks + 2):
        if j < n_chunks:
            send_xy(j)
        if 1 <= j <= n_chunks:
            multiply(j - 1)
        if j == n_chunks - 1:
            def told(x2, y2):
                q2 = x2 * ny + y2
                wait_from(note_recv.at[q2], nr_sem.at[q2], xy_at(x2, y2))

            each_xy(told)
            pltpu.make_async_copy(note_send, note_recv.at[q], nl_sem).wait()
            last_send[...] = jnp.max(note_recv[...].astype(F32), axis=0).astype(BF16)
            last = pltpu.make_async_remote_copy(
                src_ref=last_send, dst_ref=last_recv, send_sem=ls_sem, recv_sem=lr_sem,
                device_id=sibling, device_id_type=MESH,
            )
            last.start()
        if 2 <= j:
            finish(j - 2)

    last.wait()
    flag_ref[...] = jnp.maximum(last_send[...].astype(F32), last_recv[...].astype(F32))[0:8, :]
    for d in z_steps:
        meta_copy(lax.rem(z + d, nz)).wait_send()
    each_xy(lambda x2, y2: note_copy(x2, y2).wait_send())
    for j in range(n_chunks):
        for d in z_steps:
            z_copy(j, lax.rem(z + d, nz)).wait_send()
        each_xy(lambda x2, y2: xy_copy(j, x2, y2).wait_send())
        dp_copy(j).wait_send()
        out_copy(j).wait()


def fast_body(grad_out, combine, routes, tasks, task_lists, gate_up):
    n_experts = lax.axis_size("exp")
    nx, nz, ny = GRID[n_experts]
    slot_rows = gate_up.shape[1]
    cap = slot_rows // n_experts
    cap_rows = -(-(cap + 1) // 8) * 8
    room = CAPACITY[n_experts]
    tok_count, width = grad_out.shape
    chunks = tiles_of(width, CHUNK[width])
    hidden_width = gate_up.shape[2] // 2
    half = hidden_width // 2
    plane, block = nx * ny, nz * cap
    n = len(chunks)
    dma = pltpu.SemaphoreType.DMA
    each = lambda shape, kind: [pltpu.VMEM((*shape, size), kind) for _, size in chunks]
    meta = (4 * cap_rows, n_experts)
    scratch = (
        each((nz, room), BF16) + each((nz, room), BF16)
        + each((plane, block), BF16) + each((plane, block), BF16)
        + each((half,), F32) + each((half,), BF16) + each((half,), BF16) + each((half,), BF16)
        + [
            pltpu.VMEM((nz * room, tok_count), BF16),
            pltpu.VMEM((2 * hidden_width, slot_rows), BF16),
            pltpu.VMEM((hidden_width, slot_rows), BF16),
            pltpu.VMEM((slot_rows, nz * room), BF16),
            pltpu.VMEM((slot_rows, 128), F32),
            pltpu.VMEM(meta, BF16), pltpu.VMEM((nz, *meta), BF16),
            pltpu.VMEM((16, 128), BF16), pltpu.VMEM((plane, 16, 128), BF16),
            pltpu.VMEM((16, 128), BF16), pltpu.VMEM((16, 128), BF16),
            dma((n, nz)), dma((n, nz)), dma((n, plane)), dma((n, plane)),
            dma((n,)), dma((n,)), dma((n,)),
            dma((nz,)), dma((nz,)), dma((plane,)), dma((plane,)), dma, dma, dma,
            dma((n,)), dma((n,)), dma, dma,
        ]
    )
    vmem = pl.BlockSpec(memory_space=pltpu.VMEM)
    hbm = pl.BlockSpec(memory_space=pl.ANY)
    sizes = ((nx, nz, ny), cap, cap_rows, room, chunks)
    return pl.pallas_call(
        functools.partial(kernel, sizes),
        out_shape=(
            jax.ShapeDtypeStruct((half, width), BF16),
            jax.ShapeDtypeStruct((8, 128), F32),
        ),
        in_specs=[vmem] * 5 + [hbm],
        out_specs=(hbm, vmem),
        scratch_shapes=scratch,
        compiler_params=pltpu.CompilerParams(
            collective_id=0, has_side_effects=True, vmem_limit_bytes=60 * 1024 * 1024
        ),
    )(grad_out.T, combine.T, routes.T, tasks[None], task_lists, gate_up[0].T)


def body(*args):
    fast, flag = fast_body(*args)
    result = lax.cond(flag[0, 0] > 0.5, lambda a: dense_body(*a), lambda a: fast, args)
    return result[None]


def solution(mesh):
    in_specs = (
        P(("exp", "dp"), None),
        P(("exp", "dp"), None),
        P(("exp", "dp"), None),
        P(("exp", "dp")),
        P(),
        P("exp", "dp", None),
    )
    out_specs = P("exp", "dp", None)
    return jax.shard_map(body, mesh=mesh, in_specs=in_specs, out_specs=out_specs, check_vma=False)
```

```python
import functools

import jax
import jax.numpy as jnp
from jax import lax
from jax.experimental import pallas as pl
from jax.experimental.pallas import tpu as pltpu
from jax.sharding import PartitionSpec as P

F32, BF16, I32 = jnp.float32, jnp.bfloat16, jnp.int32
MESH = pl.DeviceIdType.MESH
GRID = {128: (4, 8, 4), 8: (2, 2, 2)}
CHUNKS = {2880: (256, 256, 384, 384, 384, 384, 384, 256, 192), 320: (128, 128, 64)}
HOPS = {8: (4, 3), 2: (1, 0)}


def iota(shape, dim):
    return lax.broadcasted_iota(I32, shape, dim)


def whole_part(values, step):
    return jnp.floor((values.astype(F32) + 0.5) * (1.0 / step)).astype(I32)


def dot(left, right):
    return jnp.dot(left, right, preferred_element_type=F32)


def dot_lanes(left, right):
    return lax.dot_general(left, right, (((1,), (1,)), ((), ())), preferred_element_type=F32)


def tiles_of(width, step):
    return [(start, min(step, width - start)) for start in range(0, width, step)]


def kernel(
    sizes, tok_ref, comb_ref, routes_ref, task_ref, lists_ref, gate_up_ref, out_ref, *scratch
):
    (nx, nz, ny), cap, cap_rows, chunks = sizes
    n_chunks = len(chunks)
    width, tok_count = tok_ref.shape
    double, slot_rows = gate_up_ref.shape
    hidden_width = double // 2
    half = hidden_width // 2
    experts, plane = nx * nz * ny, nx * ny
    block = nz * cap
    ahead, back = HOPS[nz]

    scratch = list(scratch)
    take = lambda count: [scratch.pop(0) for _ in range(count)]
    tokens, xy_send, xy_recv = (take(n_chunks) for _ in range(3))
    own, dp_send, dp_recv, out_buf = (take(n_chunks) for _ in range(4))
    gu, hidden, spread, weight, meta_send, meta_recv = take(6)
    as_sem, ar_sem, bs_sem, br_sem, xs_sem, xr_sem, xl_sem = take(7)
    ds_sem, dr_sem, out_sem, ms_sem, mr_sem, ml_sem, gu_sem = take(7)

    e_id, p = lax.axis_index("exp"), lax.axis_index("dp")
    y = lax.rem(e_id, ny)
    z = lax.rem(lax.div(e_id, ny), nz)
    x = lax.div(e_id, ny * nz)
    q = x * ny + y
    way = 1 - 2 * p
    z_steps = sorted(range(1, nz), key=lambda d: -min(d, nz - d))
    xy_steps = sorted(
        ((dx, dy) for dx in range(nx) for dy in range(ny) if dx or dy),
        key=lambda s: -(min(s[0], nx - s[0]) + min(s[1], ny - s[1])),
    )

    def along(hops):
        return lax.rem(z + way * hops + 2 * nz, nz)

    def z_at(z2):
        return ((x * nz + z2) * ny + y, p)

    def xy_at(x2, y2):
        return ((x2 * nz + z) * ny + y2, p)

    sibling = (e_id, 1 - p)

    gu_copy = pltpu.make_async_copy(gate_up_ref, gu, gu_sem)
    gu_copy.start()

    barrier = pltpu.get_barrier_semaphore()
    for d in z_steps:
        pl.semaphore_signal(barrier, inc=1, device_id=z_at(lax.rem(z + d, nz)), device_id_type=MESH)
    for dx, dy in xy_steps:
        pl.semaphore_signal(
            barrier, inc=1, device_id=xy_at(lax.rem(x + dx, nx), lax.rem(y + dy, ny)),
            device_id_type=MESH,
        )
    pl.semaphore_signal(barrier, inc=1, device_id=sibling, device_id_type=MESH)

    same = jnp.where(
        iota((tok_count, tok_count), 0) == iota((tok_count, tok_count), 1), 1.0, 0.0
    ).astype(BF16)

    def turn(j):
        start, size = chunks[j]
        tokens[j][z] = dot_lanes(same, tok_ref[start : start + size, :]).astype(BF16)

    def ahead_copy(j, hop):
        slot = along(-hop)
        return pltpu.make_async_remote_copy(
            src_ref=tokens[j].at[slot], dst_ref=tokens[j].at[slot],
            send_sem=as_sem.at[j, hop], recv_sem=ar_sem.at[j, hop],
            device_id=z_at(along(1)), device_id_type=MESH,
        )

    def back_copy(j, hop):
        slot = along(hop)
        return pltpu.make_async_remote_copy(
            src_ref=tokens[j].at[slot], dst_ref=tokens[j].at[slot],
            send_sem=bs_sem.at[j, hop], recv_sem=br_sem.at[j, hop],
            device_id=z_at(along(-1)), device_id_type=MESH,
        )

    def wait_from(ref, sem, device):
        pltpu.make_async_remote_copy(
            src_ref=ref, dst_ref=ref, send_sem=sem, recv_sem=sem,
            device_id=device, device_id_type=MESH,
        ).wait_recv()

    def arrive(j, hop):
        if hop < ahead:
            wait_from(tokens[j].at[along(-hop - 1)], ar_sem.at[j, hop], z_at(along(-1)))
        if hop < back:
            wait_from(tokens[j].at[along(hop + 1)], br_sem.at[j, hop], z_at(along(1)))

    def leave(j, hop):
        if hop < ahead:
            ahead_copy(j, hop).start()
        if hop < back:
            back_copy(j, hop).start()

    def forward(j, hop):
        if j < n_chunks and hop < max(ahead, back):
            arrive(j, hop - 1)
            leave(j, hop)

    def begin(j):
        if j < n_chunks:
            turn(j)
            leave(j, 0)

    turn(0)
    pl.semaphore_wait(barrier, len(z_steps) + len(xy_steps) + 1)
    leave(0, 0)
    begin(1)
    last = max(ahead, back) - 1

    def tick(t):
        for hop in range(last, 0, -1):
            if t >= hop:
                forward(t - hop, hop)
        if t:
            begin(t + 1)

    expert_col = iota((experts, tok_count), 0)
    named = jnp.zeros((experts, tok_count), F32)
    weight_of = jnp.zeros((experts, tok_count), F32)
    for k in range(routes_ref.shape[0]):
        hit = expert_col == routes_ref[k : k + 1, :]
        named = jnp.where(hit, 1.0, named)
        weight_of = jnp.where(hit, comb_ref[k : k + 1, :], weight_of)
    lists = lists_ref[...]
    of_task = iota(lists.shape, 0) == task_ref[0:1, 0:1]
    chosen = jnp.max(jnp.where(of_task, lists, -1), axis=0, keepdims=True)
    trainable = jnp.max(
        jnp.where(iota((experts, lists.shape[1]), 0) == chosen, 1.0, 0.0), axis=1, keepdims=True
    )
    before = jnp.where(
        iota((tok_count, tok_count), 0) < iota((tok_count, tok_count), 1), 1.0, 0.0
    ).astype(BF16)
    slot = dot(named.astype(BF16), before)
    live = named * trainable
    token_row = iota((experts, tok_count), 1).astype(F32) + 1.0
    meta_lane = iota((experts, 128), 1)
    meta = jnp.zeros((experts, 128), F32)
    for c in range(cap):
        here = jnp.where((slot > c - 0.5) & (slot < c + 0.5), live, 0.0)
        at = jnp.sum(here * token_row, axis=1, keepdims=True)
        w = jnp.sum(here * weight_of, axis=1, keepdims=True)
        high = w.astype(BF16).astype(F32)
        mid = (w - high).astype(BF16).astype(F32)
        for kind, value in enumerate((at, high, mid, w - high - mid)):
            meta = jnp.where(meta_lane == kind * cap_rows + c, value, meta)
    meta_send[...] = jnp.transpose(meta)[: 4 * cap_rows, :].astype(BF16)

    def meta_copy(z2):
        return pltpu.make_async_remote_copy(
            src_ref=meta_send, dst_ref=meta_recv.at[z],
            send_sem=ms_sem.at[z2], recv_sem=mr_sem.at[z],
            device_id=z_at(z2), device_id_type=MESH,
        )

    for d in z_steps:
        meta_copy(lax.rem(z + d, nz)).start()
    pltpu.make_async_copy(meta_send, meta_recv.at[z], ml_sem).start()

    step = 96 if hidden_width % 96 == 0 else 32
    pieces = hidden_width // step

    def activate(first, stop):
        @pl.loop(first, stop)
        def _(i):
            rows = pl.ds(pl.multiple_of(i * step, step), step)
            gate = gu[rows, :].astype(F32)
            up = gu[pl.ds(pl.multiple_of(i * step + hidden_width, step), step), :].astype(F32)
            gu[rows, :] = ((up + 1.0) * gate * jax.nn.sigmoid(1.702 * gate)).astype(BF16)

    def reorder():
        for start, size in tiles_of(slot_rows, 256):
            to = iota((slot_rows, size), 1) + start
            to_q = whole_part(to, block)
            rest = to - to_q * block
            to_z = whole_part(rest, cap)
            c = rest - to_z * cap
            to_x = whole_part(to_q, ny)
            source = ((to_x * nz + to_z) * ny + (to_q - to_x * ny)) * cap + c
            order = jnp.where(iota((slot_rows, size), 0) == source, 1.0, 0.0).astype(BF16)
            hidden[:, start : start + size] = dot(gu[0:hidden_width, :], order).astype(BF16)

    def place_slots():
        for d in z_steps:
            z2 = lax.rem(z + nz - d, nz)
            wait_from(meta_recv.at[z2], mr_sem.at[z2], z_at(z2))
        pltpu.make_async_copy(meta_send, meta_recv.at[z], ml_sem).wait()
        s_q = whole_part(iota((slot_rows, experts), 0), block)
        s_x = whole_part(s_q, ny)
        expert_of = (s_x * nz + z) * ny + (s_q - s_x * ny)
        at_expert = jnp.where(expert_of == iota((slot_rows, experts), 1), 1.0, 0.0).astype(BF16)
        m_col = iota((slot_rows, cap_rows * 4), 0)
        m_lane = iota((slot_rows, cap_rows * 4), 1)
        m_rest = m_col - whole_part(m_col, block) * block
        m_z = whole_part(m_rest, cap)
        m_c = m_rest - m_z * cap
        totals = jnp.zeros((slot_rows, cap_rows * 4), F32)
        for z2 in range(nz):
            totals = jnp.where(m_z == z2, dot_lanes(at_expert, meta_recv[z2]), totals)
        kind_of = whole_part(m_lane, cap_rows)
        slot_hit = m_lane - kind_of * cap_rows == m_c
        at = jnp.sum(jnp.where(slot_hit & (kind_of == 0), totals, 0.0), axis=1, keepdims=True)
        w = jnp.sum(jnp.where(slot_hit & (kind_of > 0), totals, 0.0), axis=1, keepdims=True)
        weight[...] = jnp.broadcast_to(w, weight.shape)
        r_col = iota((slot_rows, 1), 0)
        r_rest = r_col - whole_part(r_col, block) * block
        at = jnp.where(at > 0.5, at - 1.0 + (whole_part(r_rest, cap) * tok_count).astype(F32), -1.0)
        spread[...] = jnp.where(
            iota((slot_rows, nz * tok_count), 1).astype(F32) == at, 1.0, 0.0
        ).astype(BF16)

    def xy_copy(j, x2, y2):
        q2 = x2 * ny + y2
        return pltpu.make_async_remote_copy(
            src_ref=xy_send[j].at[q2], dst_ref=xy_recv[j].at[q],
            send_sem=xs_sem.at[j, q2], recv_sem=xr_sem.at[j, q],
            device_id=xy_at(x2, y2), device_id_type=MESH,
        )

    def dp_copy(j):
        return pltpu.make_async_remote_copy(
            src_ref=dp_send[j], dst_ref=dp_recv[j], send_sem=ds_sem.at[j], recv_sem=dr_sem.at[j],
            device_id=sibling, device_id_type=MESH,
        )

    def each_xy(act):
        for dx, dy in xy_steps:
            act(lax.rem(x + dx, nx), lax.rem(y + dy, ny))

    def send_xy(j):
        arrive(j, last)
        for start, part in tiles_of(chunks[j][1], 256):
            rows = tokens[j][:, :, start : start + part].reshape(nz * tok_count, part)
            by = jnp.concatenate([weight[...]] * 2, axis=1)[:, :part]
            xy_send[j][:, :, start : start + part] = (
                (dot(spread[...], rows) * by).astype(BF16).reshape(plane, block, part)
            )
        each_xy(lambda x2, y2: xy_copy(j, x2, y2).start())
        pltpu.make_async_copy(xy_send[j].at[q], xy_recv[j].at[q], xl_sem.at[j]).start()

    def multiply(j):
        def arrived(x2, y2):
            q2 = x2 * ny + y2
            wait_from(xy_recv[j].at[q2], xr_sem.at[j, q2], xy_at(x2, y2))

        each_xy(arrived)
        pltpu.make_async_copy(xy_send[j].at[q], xy_recv[j].at[q], xl_sem.at[j]).wait()
        theirs = pl.ds(pl.multiple_of((1 - p) * half, 16), half)
        mine = pl.ds(pl.multiple_of(p * half, 16), half)
        parts = tiles_of(chunks[j][1], 256)
        for start, part in parts:
            rows = xy_recv[j][:, :, start : start + part].reshape(slot_rows, part)
            dp_send[j][:, start : start + part] = dot(hidden[theirs, :], rows).astype(BF16)
        dp_copy(j).start()
        for start, part in parts:
            rows = xy_recv[j][:, :, start : start + part].reshape(slot_rows, part)
            own[j][:, start : start + part] = dot(hidden[mine, :], rows)

    def out_copy(j):
        start, size = chunks[j]
        return pltpu.make_async_copy(
            out_buf[j], out_ref.at[:, start : start + size], out_sem.at[j]
        )

    def finish(j):
        dp_copy(j).wait_recv()
        out_buf[j][...] = (own[j][...] + dp_recv[j][...].astype(F32)).astype(BF16)
        out_copy(j).start()

    third = pieces // 3
    duties = {
        1: [gu_copy.wait, lambda: activate(0, third)],
        2: [lambda: activate(third, 2 * third)],
        3: [place_slots],
        4: [lambda: activate(2 * third, pieces), reorder],
    }
    for t in range(n_chunks + last + 3):
        if t:
            tick(t)
        for when in sorted(duties):
            if when == t or (last < 3 and t == 0):
                for duty in duties[when]:
                    duty()
        if 0 <= t - last - 2 < n_chunks:
            multiply(t - last - 2)
        if 0 <= t - last < n_chunks:
            send_xy(t - last)
        if 0 <= t - last - 3:
            finish(t - last - 3)

    for d in z_steps:
        meta_copy(lax.rem(z + d, nz)).wait_send()
    for j in range(n_chunks):
        for hop in range(ahead):
            ahead_copy(j, hop).wait_send()
        for hop in range(back):
            back_copy(j, hop).wait_send()
        each_xy(lambda x2, y2: xy_copy(j, x2, y2).wait_send())
        dp_copy(j).wait_send()
        out_copy(j).wait()


def body(grad_out, combine, routes, tasks, task_lists, gate_up):
    n_experts = lax.axis_size("exp")
    nx, nz, ny = GRID[n_experts]
    slot_rows = gate_up.shape[1]
    cap = slot_rows // n_experts
    cap_rows = -(-cap // 8) * 8
    tok_count, width = grad_out.shape
    starts = [sum(CHUNKS[width][:i]) for i in range(len(CHUNKS[width]))]
    chunks = list(zip(starts, CHUNKS[width]))
    hidden_width = gate_up.shape[2] // 2
    half = hidden_width // 2
    plane, block = nx * ny, nz * cap
    n = len(chunks)
    ahead, back = HOPS[nz]
    dma = pltpu.SemaphoreType.DMA
    each = lambda shape, kind: [pltpu.VMEM((*shape, size), kind) for _, size in chunks]
    meta = (4 * cap_rows, n_experts)
    scratch = (
        each((nz, tok_count), BF16)
        + each((plane, block), BF16) + each((plane, block), BF16)
        + each((half,), F32) + each((half,), BF16) + each((half,), BF16) + each((half,), BF16)
        + [
            pltpu.VMEM((2 * hidden_width, slot_rows), BF16),
            pltpu.VMEM((hidden_width, slot_rows), BF16),
            pltpu.VMEM((slot_rows, nz * tok_count), BF16),
            pltpu.VMEM((slot_rows, 128), F32),
            pltpu.VMEM(meta, BF16), pltpu.VMEM((nz, *meta), BF16),
            dma((n, ahead)), dma((n, ahead)), dma((n, max(back, 1))), dma((n, max(back, 1))),
            dma((n, plane)), dma((n, plane)), dma((n,)),
            dma((n,)), dma((n,)), dma((n,)), dma((nz,)), dma((nz,)), dma, dma,
        ]
    )
    vmem = pl.BlockSpec(memory_space=pltpu.VMEM)
    hbm = pl.BlockSpec(memory_space=pl.ANY)
    sizes = ((nx, nz, ny), cap, cap_rows, chunks)
    return pl.pallas_call(
        functools.partial(kernel, sizes),
        out_shape=jax.ShapeDtypeStruct((half, width), BF16),
        in_specs=[vmem] * 5 + [hbm],
        out_specs=hbm,
        scratch_shapes=scratch,
        compiler_params=pltpu.CompilerParams(
            collective_id=0, has_side_effects=True, vmem_limit_bytes=60 * 1024 * 1024
        ),
    )(grad_out.T, combine.T, routes.T, tasks[None], task_lists, gate_up[0].T)[None]


def solution(mesh):
    in_specs = (
        P(("exp", "dp"), None),
        P(("exp", "dp"), None),
        P(("exp", "dp"), None),
        P(("exp", "dp")),
        P(),
        P("exp", "dp", None),
    )
    out_specs = P("exp", "dp", None)
    return jax.shard_map(body, mesh=mesh, in_specs=in_specs, out_specs=out_specs, check_vma=False)
```

```python
import functools

import jax
import jax.numpy as jnp
from jax import lax
from jax.experimental import pallas as pl
from jax.experimental.pallas import tpu as pltpu
from jax.sharding import PartitionSpec as P

F32, BF16, I32 = jnp.float32, jnp.bfloat16, jnp.int32
MESH = pl.DeviceIdType.MESH
GRID = {128: (4, 8, 4), 8: (2, 2, 2)}
CHUNKS = {2880: (256, 256, 384, 384, 384, 384, 384, 256, 192), 320: (128, 128, 64)}
HOPS = {8: (4, 3), 2: (1, 0)}


def iota(shape, dim):
    return lax.broadcasted_iota(I32, shape, dim)


def whole_part(values, step):
    return jnp.floor((values.astype(F32) + 0.5) * (1.0 / step)).astype(I32)


def dot(left, right):
    return jnp.dot(left, right, preferred_element_type=F32)


def dot_lanes(left, right):
    return lax.dot_general(left, right, (((1,), (1,)), ((), ())), preferred_element_type=F32)


def tiles_of(width, step):
    return [(start, min(step, width - start)) for start in range(0, width, step)]


def kernel(
    sizes, tok_ref, comb_ref, routes_ref, task_ref, lists_ref, gate_up_ref, out_ref, *scratch
):
    (nx, nz, ny), cap, cap_rows, chunks = sizes
    n_chunks = len(chunks)
    width, tok_count = tok_ref.shape
    double, slot_rows = gate_up_ref.shape
    hidden_width = double // 2
    half = hidden_width // 2
    experts, plane = nx * nz * ny, nx * ny
    block = nz * cap
    ahead, back = HOPS[nz]

    scratch = list(scratch)
    take = lambda count: [scratch.pop(0) for _ in range(count)]
    tokens, xy_send, xy_recv = (take(n_chunks) for _ in range(3))
    own, dp_send, dp_recv, out_buf = (take(n_chunks) for _ in range(4))
    gu, hidden, spread, weight, meta_send, meta_recv = take(6)
    as_sem, ar_sem, bs_sem, br_sem, xs_sem, xr_sem, xl_sem = take(7)
    ds_sem, dr_sem, out_sem, ms_sem, mr_sem, ml_sem, gu_sem = take(7)

    e_id, p = lax.axis_index("exp"), lax.axis_index("dp")
    y = lax.rem(e_id, ny)
    z = lax.rem(lax.div(e_id, ny), nz)
    x = lax.div(e_id, ny * nz)
    q = x * ny + y
    way = 1 - 2 * p
    z_steps = sorted(range(1, nz), key=lambda d: -min(d, nz - d))
    xy_steps = sorted(
        ((dx, dy) for dx in range(nx) for dy in range(ny) if dx or dy),
        key=lambda s: -(min(s[0], nx - s[0]) + min(s[1], ny - s[1])),
    )

    def along(hops):
        return lax.rem(z + way * hops + 2 * nz, nz)

    def z_at(z2):
        return ((x * nz + z2) * ny + y, p)

    def xy_at(x2, y2):
        return ((x2 * nz + z) * ny + y2, p)

    sibling = (e_id, 1 - p)

    gu_copy = pltpu.make_async_copy(gate_up_ref, gu, gu_sem)
    gu_copy.start()

    barrier = pltpu.get_barrier_semaphore()
    for d in z_steps:
        pl.semaphore_signal(barrier, inc=1, device_id=z_at(lax.rem(z + d, nz)), device_id_type=MESH)
    for dx, dy in xy_steps:
        pl.semaphore_signal(
            barrier, inc=1, device_id=xy_at(lax.rem(x + dx, nx), lax.rem(y + dy, ny)),
            device_id_type=MESH,
        )
    pl.semaphore_signal(barrier, inc=1, device_id=sibling, device_id_type=MESH)

    same = jnp.where(
        iota((tok_count, tok_count), 0) == iota((tok_count, tok_count), 1), 1.0, 0.0
    ).astype(BF16)

    def turn(j):
        start, size = chunks[j]
        tokens[j][z] = dot_lanes(same, tok_ref[start : start + size, :]).astype(BF16)

    def ahead_copy(j, hop):
        slot = along(-hop)
        return pltpu.make_async_remote_copy(
            src_ref=tokens[j].at[slot], dst_ref=tokens[j].at[slot],
            send_sem=as_sem.at[j, hop], recv_sem=ar_sem.at[j, hop],
            device_id=z_at(along(1)), device_id_type=MESH,
        )

    def back_copy(j, hop):
        slot = along(hop)
        return pltpu.make_async_remote_copy(
            src_ref=tokens[j].at[slot], dst_ref=tokens[j].at[slot],
            send_sem=bs_sem.at[j, hop], recv_sem=br_sem.at[j, hop],
            device_id=z_at(along(-1)), device_id_type=MESH,
        )

    def wait_from(ref, sem, device):
        pltpu.make_async_remote_copy(
            src_ref=ref, dst_ref=ref, send_sem=sem, recv_sem=sem,
            device_id=device, device_id_type=MESH,
        ).wait_recv()

    def arrive(j, hop):
        if hop < ahead:
            wait_from(tokens[j].at[along(-hop - 1)], ar_sem.at[j, hop], z_at(along(-1)))
        if hop < back:
            wait_from(tokens[j].at[along(hop + 1)], br_sem.at[j, hop], z_at(along(1)))

    def leave(j, hop):
        if hop < ahead:
            ahead_copy(j, hop).start()
        if hop < back:
            back_copy(j, hop).start()

    def forward(j, hop):
        if j < n_chunks and hop < max(ahead, back):
            arrive(j, hop - 1)
            leave(j, hop)

    def begin(j):
        if j < n_chunks:
            turn(j)
            leave(j, 0)

    turn(0)
    pl.semaphore_wait(barrier, len(z_steps) + len(xy_steps) + 1)
    leave(0, 0)
    begin(1)
    last = max(ahead, back) - 1

    def tick(t):
        for hop in range(last, 0, -1):
            if t >= hop:
                forward(t - hop, hop)
        if t:
            begin(t + 1)

    expert_col = iota((experts, tok_count), 0)
    named = jnp.zeros((experts, tok_count), F32)
    weight_of = jnp.zeros((experts, tok_count), F32)
    for k in range(routes_ref.shape[0]):
        hit = expert_col == routes_ref[k : k + 1, :]
        named = jnp.where(hit, 1.0, named)
        weight_of = jnp.where(hit, comb_ref[k : k + 1, :], weight_of)
    lists = lists_ref[...]
    of_task = iota(lists.shape, 0) == task_ref[0:1, 0:1]
    chosen = jnp.max(jnp.where(of_task, lists, -1), axis=0, keepdims=True)
    trainable = jnp.max(
        jnp.where(iota((experts, lists.shape[1]), 0) == chosen, 1.0, 0.0), axis=1, keepdims=True
    )
    before = jnp.where(
        iota((tok_count, tok_count), 0) < iota((tok_count, tok_count), 1), 1.0, 0.0
    ).astype(BF16)
    slot = dot(named.astype(BF16), before)
    live = named * trainable
    token_row = iota((experts, tok_count), 1).astype(F32) + 1.0
    meta_lane = iota((experts, 128), 1)
    meta = jnp.zeros((experts, 128), F32)
    for c in range(cap):
        here = jnp.where((slot > c - 0.5) & (slot < c + 0.5), live, 0.0)
        at = jnp.sum(here * token_row, axis=1, keepdims=True)
        w = jnp.sum(here * weight_of, axis=1, keepdims=True)
        high = w.astype(BF16).astype(F32)
        mid = (w - high).astype(BF16).astype(F32)
        for kind, value in enumerate((at, high, mid, w - high - mid)):
            meta = jnp.where(meta_lane == kind * cap_rows + c, value, meta)
    meta_send[...] = jnp.transpose(meta)[: 4 * cap_rows, :].astype(BF16)

    def meta_copy(z2):
        return pltpu.make_async_remote_copy(
            src_ref=meta_send, dst_ref=meta_recv.at[z],
            send_sem=ms_sem.at[z2], recv_sem=mr_sem.at[z],
            device_id=z_at(z2), device_id_type=MESH,
        )

    for d in z_steps:
        meta_copy(lax.rem(z + d, nz)).start()
    pltpu.make_async_copy(meta_send, meta_recv.at[z], ml_sem).start()

    step = 96 if hidden_width % 96 == 0 else 32
    pieces = hidden_width // step

    def activate(first, stop):
        @pl.loop(first, stop)
        def _(i):
            rows = pl.ds(pl.multiple_of(i * step, step), step)
            gate = gu[rows, :].astype(F32)
            up = gu[pl.ds(pl.multiple_of(i * step + hidden_width, step), step), :].astype(F32)
            gu[rows, :] = ((up + 1.0) * gate * jax.nn.sigmoid(1.702 * gate)).astype(BF16)

    def reorder():
        for start, size in tiles_of(slot_rows, 256):
            to = iota((slot_rows, size), 1) + start
            to_q = whole_part(to, block)
            rest = to - to_q * block
            to_z = whole_part(rest, cap)
            c = rest - to_z * cap
            to_x = whole_part(to_q, ny)
            source = ((to_x * nz + to_z) * ny + (to_q - to_x * ny)) * cap + c
            order = jnp.where(iota((slot_rows, size), 0) == source, 1.0, 0.0).astype(BF16)
            hidden[:, start : start + size] = dot(gu[0:hidden_width, :], order).astype(BF16)

    def place_slots():
        for d in z_steps:
            z2 = lax.rem(z + nz - d, nz)
            wait_from(meta_recv.at[z2], mr_sem.at[z2], z_at(z2))
        pltpu.make_async_copy(meta_send, meta_recv.at[z], ml_sem).wait()
        s_q = whole_part(iota((slot_rows, experts), 0), block)
        s_x = whole_part(s_q, ny)
        expert_of = (s_x * nz + z) * ny + (s_q - s_x * ny)
        at_expert = jnp.where(expert_of == iota((slot_rows, experts), 1), 1.0, 0.0).astype(BF16)
        m_col = iota((slot_rows, cap_rows * 4), 0)
        m_lane = iota((slot_rows, cap_rows * 4), 1)
        m_rest = m_col - whole_part(m_col, block) * block
        m_z = whole_part(m_rest, cap)
        m_c = m_rest - m_z * cap
        totals = jnp.zeros((slot_rows, cap_rows * 4), F32)
        for z2 in range(nz):
            totals = jnp.where(m_z == z2, dot_lanes(at_expert, meta_recv[z2]), totals)
        kind_of = whole_part(m_lane, cap_rows)
        slot_hit = m_lane - kind_of * cap_rows == m_c
        at = jnp.sum(jnp.where(slot_hit & (kind_of == 0), totals, 0.0), axis=1, keepdims=True)
        w = jnp.sum(jnp.where(slot_hit & (kind_of > 0), totals, 0.0), axis=1, keepdims=True)
        weight[...] = jnp.broadcast_to(w, weight.shape)
        r_col = iota((slot_rows, 1), 0)
        r_rest = r_col - whole_part(r_col, block) * block
        at = jnp.where(at > 0.5, at - 1.0 + (whole_part(r_rest, cap) * tok_count).astype(F32), -1.0)
        spread[...] = jnp.where(
            iota((slot_rows, nz * tok_count), 1).astype(F32) == at, 1.0, 0.0
        ).astype(BF16)

    def xy_copy(j, x2, y2):
        q2 = x2 * ny + y2
        return pltpu.make_async_remote_copy(
            src_ref=xy_send[j].at[q2], dst_ref=xy_recv[j].at[q],
            send_sem=xs_sem.at[j, q2], recv_sem=xr_sem.at[j, q],
            device_id=xy_at(x2, y2), device_id_type=MESH,
        )

    def dp_copy(j):
        return pltpu.make_async_remote_copy(
            src_ref=dp_send[j], dst_ref=dp_recv[j], send_sem=ds_sem.at[j], recv_sem=dr_sem.at[j],
            device_id=sibling, device_id_type=MESH,
        )

    def each_xy(act):
        for dx, dy in xy_steps:
            act(lax.rem(x + dx, nx), lax.rem(y + dy, ny))

    def send_xy(j):
        arrive(j, last)
        for start, part in tiles_of(chunks[j][1], 256):
            rows = tokens[j][:, :, start : start + part].reshape(nz * tok_count, part)
            by = jnp.concatenate([weight[...]] * 2, axis=1)[:, :part]
            xy_send[j][:, :, start : start + part] = (
                (dot(spread[...], rows) * by).astype(BF16).reshape(plane, block, part)
            )
        each_xy(lambda x2, y2: xy_copy(j, x2, y2).start())
        pltpu.make_async_copy(xy_send[j].at[q], xy_recv[j].at[q], xl_sem.at[j]).start()

    def multiply(j):
        def arrived(x2, y2):
            q2 = x2 * ny + y2
            wait_from(xy_recv[j].at[q2], xr_sem.at[j, q2], xy_at(x2, y2))

        each_xy(arrived)
        pltpu.make_async_copy(xy_send[j].at[q], xy_recv[j].at[q], xl_sem.at[j]).wait()
        theirs = pl.ds(pl.multiple_of((1 - p) * half, 16), half)
        mine = pl.ds(pl.multiple_of(p * half, 16), half)
        parts = tiles_of(chunks[j][1], 256)
        for start, part in parts:
            rows = xy_recv[j][:, :, start : start + part].reshape(slot_rows, part)
            dp_send[j][:, start : start + part] = dot(hidden[theirs, :], rows).astype(BF16)
        dp_copy(j).start()
        for start, part in parts:
            rows = xy_recv[j][:, :, start : start + part].reshape(slot_rows, part)
            own[j][:, start : start + part] = dot(hidden[mine, :], rows)

    def out_copy(j):
        start, size = chunks[j]
        return pltpu.make_async_copy(
            out_buf[j], out_ref.at[:, start : start + size], out_sem.at[j]
        )

    def finish(j):
        dp_copy(j).wait_recv()
        out_buf[j][...] = (own[j][...] + dp_recv[j][...].astype(F32)).astype(BF16)
        out_copy(j).start()

    third = pieces // 3
    duties = {
        1: [gu_copy.wait, lambda: activate(0, third)],
        2: [lambda: activate(third, 2 * third)],
        3: [place_slots],
        4: [lambda: activate(2 * third, pieces), reorder],
    }
    for t in range(n_chunks + last + 4):
        if t:
            tick(t)
        for when in sorted(duties):
            if when == t or (last < 3 and t == 0):
                for duty in duties[when]:
                    duty()
        if 0 <= t - last - 3 < n_chunks:
            multiply(t - last - 3)
        if 0 <= t - last < n_chunks:
            send_xy(t - last)
        if 0 <= t - last - 4:
            finish(t - last - 4)

    for d in z_steps:
        meta_copy(lax.rem(z + d, nz)).wait_send()
    for j in range(n_chunks):
        for hop in range(ahead):
            ahead_copy(j, hop).wait_send()
        for hop in range(back):
            back_copy(j, hop).wait_send()
        each_xy(lambda x2, y2: xy_copy(j, x2, y2).wait_send())
        dp_copy(j).wait_send()
        out_copy(j).wait()


def hand_over(held_ref, out_ref, pieces, in_sems, out_sems):
    rows = pieces.shape[1]
    parts = [pl.ds(i * rows, rows) for i in range(pieces.shape[0])]
    ins = [pltpu.make_async_copy(held_ref.at[r], pieces.at[i], in_sems.at[i]) for i, r in enumerate(parts)]
    outs = [pltpu.make_async_copy(pieces.at[i], out_ref.at[r], out_sems.at[i]) for i, r in enumerate(parts)]
    for copy in ins:
        copy.start()
    for copy, then in zip(ins, outs):
        copy.wait()
        then.start()
    for copy in outs:
        copy.wait()


def body(grad_out, combine, routes, tasks, task_lists, gate_up):
    n_experts = lax.axis_size("exp")
    nx, nz, ny = GRID[n_experts]
    slot_rows = gate_up.shape[1]
    cap = slot_rows // n_experts
    cap_rows = -(-cap // 8) * 8
    tok_count, width = grad_out.shape
    starts = [sum(CHUNKS[width][:i]) for i in range(len(CHUNKS[width]))]
    chunks = list(zip(starts, CHUNKS[width]))
    hidden_width = gate_up.shape[2] // 2
    half = hidden_width // 2
    plane, block = nx * ny, nz * cap
    n = len(chunks)
    ahead, back = HOPS[nz]
    dma = pltpu.SemaphoreType.DMA
    each = lambda shape, kind: [pltpu.VMEM((*shape, size), kind) for _, size in chunks]
    meta = (4 * cap_rows, n_experts)
    scratch = (
        each((nz, tok_count), BF16)
        + each((plane, block), BF16) + each((plane, block), BF16)
        + each((half,), F32) + each((half,), BF16) + each((half,), BF16) + each((half,), BF16)
        + [
            pltpu.VMEM((2 * hidden_width, slot_rows), BF16),
            pltpu.VMEM((hidden_width, slot_rows), BF16),
            pltpu.VMEM((slot_rows, nz * tok_count), BF16),
            pltpu.VMEM((slot_rows, 128), F32),
            pltpu.VMEM(meta, BF16), pltpu.VMEM((nz, *meta), BF16),
            dma((n, ahead)), dma((n, ahead)), dma((n, max(back, 1))), dma((n, max(back, 1))),
            dma((n, plane)), dma((n, plane)), dma((n,)),
            dma((n,)), dma((n,)), dma((n,)), dma((nz,)), dma((nz,)), dma, dma,
        ]
    )
    vmem = pl.BlockSpec(memory_space=pltpu.VMEM)
    hbm = pl.BlockSpec(memory_space=pl.ANY)
    sizes = ((nx, nz, ny), cap, cap_rows, chunks)
    result = pl.pallas_call(
        functools.partial(kernel, sizes),
        out_shape=jax.ShapeDtypeStruct((half, width), BF16),
        in_specs=[vmem] * 5 + [hbm],
        out_specs=hbm,
        scratch_shapes=scratch,
        compiler_params=pltpu.CompilerParams(
            collective_id=0, has_side_effects=True, vmem_limit_bytes=60 * 1024 * 1024
        ),
    )(grad_out.T, combine.T, routes.T, tasks[None], task_lists, gate_up[0].T)
    parts = 9 if half % 144 == 0 else 1
    return pl.pallas_call(
        hand_over,
        out_shape=jax.ShapeDtypeStruct((half, width), BF16),
        in_specs=[hbm],
        out_specs=hbm,
        scratch_shapes=[pltpu.VMEM((parts, half // parts, width), BF16), dma((parts,)), dma((parts,))],
        compiler_params=pltpu.CompilerParams(vmem_limit_bytes=60 * 1024 * 1024),
    )(result)[None]


def solution(mesh):
    in_specs = (
        P(("exp", "dp"), None),
        P(("exp", "dp"), None),
        P(("exp", "dp"), None),
        P(("exp", "dp")),
        P(),
        P("exp", "dp", None),
    )
    out_specs = P("exp", "dp", None)
    return jax.shard_map(body, mesh=mesh, in_specs=in_specs, out_specs=out_specs, check_vma=False)
```

```python
import functools

import jax
import jax.numpy as jnp
from jax import lax
from jax.experimental import pallas as pl
from jax.experimental.pallas import tpu as pltpu
from jax.sharding import PartitionSpec as P

F32, BF16, I32 = jnp.float32, jnp.bfloat16, jnp.int32
MESH = pl.DeviceIdType.MESH
GRID = {128: (4, 8, 4), 8: (2, 2, 2)}
CHUNKS = {2880: (256, 256, 384, 384, 384, 384, 384, 256, 192), 320: (128, 128, 64)}
HOPS = {8: (4, 3), 2: (1, 0)}


def iota(shape, dim):
    return lax.broadcasted_iota(I32, shape, dim)


def whole_part(values, step):
    return jnp.floor((values.astype(F32) + 0.5) * (1.0 / step)).astype(I32)


def dot(left, right):
    return jnp.dot(left, right, preferred_element_type=F32)


def dot_lanes(left, right):
    return lax.dot_general(left, right, (((1,), (1,)), ((), ())), preferred_element_type=F32)


def tiles_of(width, step):
    return [(start, min(step, width - start)) for start in range(0, width, step)]


def kernel(
    sizes, tok_ref, comb_ref, routes_ref, task_ref, lists_ref, gate_up_ref, out_ref, *scratch
):
    (nx, nz, ny), cap, cap_rows, chunks = sizes
    n_chunks = len(chunks)
    width, tok_count = tok_ref.shape
    double, slot_rows = gate_up_ref.shape
    hidden_width = double // 2
    half = hidden_width // 2
    experts, plane = nx * nz * ny, nx * ny
    block = nz * cap
    ahead, back = HOPS[nz]

    scratch = list(scratch)
    take = lambda count: [scratch.pop(0) for _ in range(count)]
    tokens, xy_send, xy_recv = (take(n_chunks) for _ in range(3))
    own, dp_send, dp_recv, out_buf = (take(n_chunks) for _ in range(4))
    gu, hidden, spread, weight, meta_send, meta_recv = take(6)
    as_sem, ar_sem, bs_sem, br_sem, xs_sem, xr_sem, xl_sem = take(7)
    ds_sem, dr_sem, out_sem, ms_sem, mr_sem, ml_sem, gu_sem = take(7)

    e_id, p = lax.axis_index("exp"), lax.axis_index("dp")
    y = lax.rem(e_id, ny)
    z = lax.rem(lax.div(e_id, ny), nz)
    x = lax.div(e_id, ny * nz)
    q = x * ny + y
    way = 1 - 2 * p
    z_steps = sorted(range(1, nz), key=lambda d: -min(d, nz - d))
    xy_steps = sorted(
        ((dx, dy) for dx in range(nx) for dy in range(ny) if dx or dy),
        key=lambda s: -(min(s[0], nx - s[0]) + min(s[1], ny - s[1])),
    )

    def along(hops):
        return lax.rem(z + way * hops + 2 * nz, nz)

    def z_at(z2):
        return ((x * nz + z2) * ny + y, p)

    def xy_at(x2, y2):
        return ((x2 * nz + z) * ny + y2, p)

    sibling = (e_id, 1 - p)

    gu_copy = pltpu.make_async_copy(gate_up_ref, gu, gu_sem)
    gu_copy.start()

    barrier = pltpu.get_barrier_semaphore()
    for d in z_steps:
        pl.semaphore_signal(barrier, inc=1, device_id=z_at(lax.rem(z + d, nz)), device_id_type=MESH)
    for dx, dy in xy_steps:
        pl.semaphore_signal(
            barrier, inc=1, device_id=xy_at(lax.rem(x + dx, nx), lax.rem(y + dy, ny)),
            device_id_type=MESH,
        )
    pl.semaphore_signal(barrier, inc=1, device_id=sibling, device_id_type=MESH)

    same = jnp.where(
        iota((tok_count, tok_count), 0) == iota((tok_count, tok_count), 1), 1.0, 0.0
    ).astype(BF16)

    def turn(j):
        start, size = chunks[j]
        tokens[j][z] = dot_lanes(same, tok_ref[start : start + size, :]).astype(BF16)

    def ahead_copy(j, hop):
        slot = along(-hop)
        return pltpu.make_async_remote_copy(
            src_ref=tokens[j].at[slot], dst_ref=tokens[j].at[slot],
            send_sem=as_sem.at[j, hop], recv_sem=ar_sem.at[j, hop],
            device_id=z_at(along(1)), device_id_type=MESH,
        )

    def back_copy(j, hop):
        slot = along(hop)
        return pltpu.make_async_remote_copy(
            src_ref=tokens[j].at[slot], dst_ref=tokens[j].at[slot],
            send_sem=bs_sem.at[j, hop], recv_sem=br_sem.at[j, hop],
            device_id=z_at(along(-1)), device_id_type=MESH,
        )

    def wait_from(ref, sem, device):
        pltpu.make_async_remote_copy(
            src_ref=ref, dst_ref=ref, send_sem=sem, recv_sem=sem,
            device_id=device, device_id_type=MESH,
        ).wait_recv()

    def ahead_in(j, hop):
        wait_from(tokens[j].at[along(-hop - 1)], ar_sem.at[j, hop], z_at(along(-1)))

    def back_in(j, hop):
        wait_from(tokens[j].at[along(hop + 1)], br_sem.at[j, hop], z_at(along(1)))

    def forward(j, hop):
        if j < n_chunks and hop < ahead:
            ahead_in(j, hop - 1)
            ahead_copy(j, hop).start()
        if j < n_chunks and hop < back:
            back_in(j, hop - 1)
            back_copy(j, hop).start()

    def arrive(j):
        if back:
            back_in(j, back - 1)
        ahead_in(j, ahead - 1)

    def leave(j):
        ahead_copy(j, 0).start()
        if back:
            back_copy(j, 0).start()

    def begin(j):
        if j < n_chunks:
            turn(j)
            leave(j)

    turn(0)
    pl.semaphore_wait(barrier, len(z_steps) + len(xy_steps) + 1)
    leave(0)
    begin(1)
    last = max(ahead, back) - 1

    def tick(t):
        for hop in range(last, 0, -1):
            if t >= hop:
                forward(t - hop, hop)
        if t:
            begin(t + 1)

    expert_col = iota((experts, tok_count), 0)
    named = jnp.zeros((experts, tok_count), F32)
    weight_of = jnp.zeros((experts, tok_count), F32)
    for k in range(routes_ref.shape[0]):
        hit = expert_col == routes_ref[k : k + 1, :]
        named = jnp.where(hit, 1.0, named)
        weight_of = jnp.where(hit, comb_ref[k : k + 1, :], weight_of)
    lists = lists_ref[...]
    of_task = iota(lists.shape, 0) == task_ref[0:1, 0:1]
    chosen = jnp.max(jnp.where(of_task, lists, -1), axis=0, keepdims=True)
    trainable = jnp.max(
        jnp.where(iota((experts, lists.shape[1]), 0) == chosen, 1.0, 0.0), axis=1, keepdims=True
    )
    before = jnp.where(
        iota((tok_count, tok_count), 0) < iota((tok_count, tok_count), 1), 1.0, 0.0
    ).astype(BF16)
    slot = dot(named.astype(BF16), before)
    live = named * trainable
    token_row = iota((experts, tok_count), 1).astype(F32) + 1.0
    meta_lane = iota((experts, 128), 1)
    meta = jnp.zeros((experts, 128), F32)
    for c in range(cap):
        here = jnp.where((slot > c - 0.5) & (slot < c + 0.5), live, 0.0)
        at = jnp.sum(here * token_row, axis=1, keepdims=True)
        w = jnp.sum(here * weight_of, axis=1, keepdims=True)
        high = w.astype(BF16).astype(F32)
        mid = (w - high).astype(BF16).astype(F32)
        for kind, value in enumerate((at, high, mid, w - high - mid)):
            meta = jnp.where(meta_lane == kind * cap_rows + c, value, meta)
    meta_send[...] = jnp.transpose(meta)[: 4 * cap_rows, :].astype(BF16)

    def meta_copy(z2):
        return pltpu.make_async_remote_copy(
            src_ref=meta_send, dst_ref=meta_recv.at[z],
            send_sem=ms_sem.at[z2], recv_sem=mr_sem.at[z],
            device_id=z_at(z2), device_id_type=MESH,
        )

    for d in z_steps:
        meta_copy(lax.rem(z + d, nz)).start()
    pltpu.make_async_copy(meta_send, meta_recv.at[z], ml_sem).start()

    step = 96 if hidden_width % 96 == 0 else 32
    pieces = hidden_width // step

    def activate(first, stop):
        @pl.loop(first, stop)
        def _(i):
            rows = pl.ds(pl.multiple_of(i * step, step), step)
            gate = gu[rows, :].astype(F32)
            up = gu[pl.ds(pl.multiple_of(i * step + hidden_width, step), step), :].astype(F32)
            gu[rows, :] = ((up + 1.0) * gate * jax.nn.sigmoid(1.702 * gate)).astype(BF16)

    def reorder():
        for start, size in tiles_of(slot_rows, 256):
            to = iota((slot_rows, size), 1) + start
            to_q = whole_part(to, block)
            rest = to - to_q * block
            to_z = whole_part(rest, cap)
            c = rest - to_z * cap
            to_x = whole_part(to_q, ny)
            source = ((to_x * nz + to_z) * ny + (to_q - to_x * ny)) * cap + c
            order = jnp.where(iota((slot_rows, size), 0) == source, 1.0, 0.0).astype(BF16)
            hidden[:, start : start + size] = dot(gu[0:hidden_width, :], order).astype(BF16)

    def place_slots():
        for d in z_steps:
            z2 = lax.rem(z + nz - d, nz)
            wait_from(meta_recv.at[z2], mr_sem.at[z2], z_at(z2))
        pltpu.make_async_copy(meta_send, meta_recv.at[z], ml_sem).wait()
        s_q = whole_part(iota((slot_rows, experts), 0), block)
        s_x = whole_part(s_q, ny)
        expert_of = (s_x * nz + z) * ny + (s_q - s_x * ny)
        at_expert = jnp.where(expert_of == iota((slot_rows, experts), 1), 1.0, 0.0).astype(BF16)
        m_col = iota((slot_rows, cap_rows * 4), 0)
        m_lane = iota((slot_rows, cap_rows * 4), 1)
        m_rest = m_col - whole_part(m_col, block) * block
        m_z = whole_part(m_rest, cap)
        m_c = m_rest - m_z * cap
        totals = jnp.zeros((slot_rows, cap_rows * 4), F32)
        for z2 in range(nz):
            totals = jnp.where(m_z == z2, dot_lanes(at_expert, meta_recv[z2]), totals)
        kind_of = whole_part(m_lane, cap_rows)
        slot_hit = m_lane - kind_of * cap_rows == m_c
        at = jnp.sum(jnp.where(slot_hit & (kind_of == 0), totals, 0.0), axis=1, keepdims=True)
        w = jnp.sum(jnp.where(slot_hit & (kind_of > 0), totals, 0.0), axis=1, keepdims=True)
        weight[...] = jnp.broadcast_to(w, weight.shape)
        r_col = iota((slot_rows, 1), 0)
        r_rest = r_col - whole_part(r_col, block) * block
        at = jnp.where(at > 0.5, at - 1.0 + (whole_part(r_rest, cap) * tok_count).astype(F32), -1.0)
        spread[...] = jnp.where(
            iota((slot_rows, nz * tok_count), 1).astype(F32) == at, 1.0, 0.0
        ).astype(BF16)

    def xy_copy(j, x2, y2):
        q2 = x2 * ny + y2
        return pltpu.make_async_remote_copy(
            src_ref=xy_send[j].at[q2], dst_ref=xy_recv[j].at[q],
            send_sem=xs_sem.at[j, q2], recv_sem=xr_sem.at[j, q],
            device_id=xy_at(x2, y2), device_id_type=MESH,
        )

    def dp_copy(j):
        return pltpu.make_async_remote_copy(
            src_ref=dp_send[j], dst_ref=dp_recv[j], send_sem=ds_sem.at[j], recv_sem=dr_sem.at[j],
            device_id=sibling, device_id_type=MESH,
        )

    def each_xy(act):
        for dx, dy in xy_steps:
            act(lax.rem(x + dx, nx), lax.rem(y + dy, ny))

    def send_xy(j):
        arrive(j)
        for start, part in tiles_of(chunks[j][1], 256):
            rows = tokens[j][:, :, start : start + part].reshape(nz * tok_count, part)
            by = jnp.concatenate([weight[...]] * 2, axis=1)[:, :part]
            xy_send[j][:, :, start : start + part] = (
                (dot(spread[...], rows) * by).astype(BF16).reshape(plane, block, part)
            )
        each_xy(lambda x2, y2: xy_copy(j, x2, y2).start())
        pltpu.make_async_copy(xy_send[j].at[q], xy_recv[j].at[q], xl_sem.at[j]).start()

    def multiply(j):
        def arrived(x2, y2):
            q2 = x2 * ny + y2
            wait_from(xy_recv[j].at[q2], xr_sem.at[j, q2], xy_at(x2, y2))

        each_xy(arrived)
        pltpu.make_async_copy(xy_send[j].at[q], xy_recv[j].at[q], xl_sem.at[j]).wait()
        theirs = pl.ds(pl.multiple_of((1 - p) * half, 16), half)
        mine = pl.ds(pl.multiple_of(p * half, 16), half)
        parts = tiles_of(chunks[j][1], 256)
        for start, part in parts:
            rows = xy_recv[j][:, :, start : start + part].reshape(slot_rows, part)
            dp_send[j][:, start : start + part] = dot(hidden[theirs, :], rows).astype(BF16)
        dp_copy(j).start()
        for start, part in parts:
            rows = xy_recv[j][:, :, start : start + part].reshape(slot_rows, part)
            own[j][:, start : start + part] = dot(hidden[mine, :], rows)

    def out_copy(j):
        start, size = chunks[j]
        return pltpu.make_async_copy(
            out_buf[j], out_ref.at[:, start : start + size], out_sem.at[j]
        )

    def finish(j):
        dp_copy(j).wait_recv()
        out_buf[j][...] = (own[j][...] + dp_recv[j][...].astype(F32)).astype(BF16)
        out_copy(j).start()

    third = pieces // 3
    duties = {
        1: [gu_copy.wait, lambda: activate(0, third)],
        2: [place_slots],
        3: [],
        4: [lambda: activate(third, 2 * third)],
        5: [lambda: activate(2 * third, pieces), reorder],
    }
    for t in range(n_chunks + last + 4):
        if t:
            tick(t)
        for when in sorted(duties):
            if when == t or (last < 3 and t == 0):
                for duty in duties[when]:
                    duty()
        if 0 <= t - last - 4:
            finish(t - last - 4)
        if 0 <= t - last - 3 < n_chunks:
            multiply(t - last - 3)
        if 0 <= t - last < n_chunks:
            send_xy(t - last)

    for d in z_steps:
        meta_copy(lax.rem(z + d, nz)).wait_send()
    for j in range(n_chunks):
        for hop in range(ahead):
            ahead_copy(j, hop).wait_send()
        for hop in range(back):
            back_copy(j, hop).wait_send()
        each_xy(lambda x2, y2: xy_copy(j, x2, y2).wait_send())
        dp_copy(j).wait_send()
        out_copy(j).wait()


def hand_over(held_ref, out_ref, pieces, in_sems, out_sems):
    rows = pieces.shape[1]
    parts = [pl.ds(i * rows, rows) for i in range(pieces.shape[0])]
    ins = [pltpu.make_async_copy(held_ref.at[r], pieces.at[i], in_sems.at[i]) for i, r in enumerate(parts)]
    outs = [pltpu.make_async_copy(pieces.at[i], out_ref.at[r], out_sems.at[i]) for i, r in enumerate(parts)]
    for copy in ins:
        copy.start()
    for copy, then in zip(ins, outs):
        copy.wait()
        then.start()
    for copy in outs:
        copy.wait()


def body(grad_out, combine, routes, tasks, task_lists, gate_up):
    n_experts = lax.axis_size("exp")
    nx, nz, ny = GRID[n_experts]
    slot_rows = gate_up.shape[1]
    cap = slot_rows // n_experts
    cap_rows = -(-cap // 8) * 8
    tok_count, width = grad_out.shape
    starts = [sum(CHUNKS[width][:i]) for i in range(len(CHUNKS[width]))]
    chunks = list(zip(starts, CHUNKS[width]))
    hidden_width = gate_up.shape[2] // 2
    half = hidden_width // 2
    plane, block = nx * ny, nz * cap
    n = len(chunks)
    ahead, back = HOPS[nz]
    dma = pltpu.SemaphoreType.DMA
    each = lambda shape, kind: [pltpu.VMEM((*shape, size), kind) for _, size in chunks]
    meta = (4 * cap_rows, n_experts)
    scratch = (
        each((nz, tok_count), BF16)
        + each((plane, block), BF16) + each((plane, block), BF16)
        + each((half,), F32) + each((half,), BF16) + each((half,), BF16) + each((half,), BF16)
        + [
            pltpu.VMEM((2 * hidden_width, slot_rows), BF16),
            pltpu.VMEM((hidden_width, slot_rows), BF16),
            pltpu.VMEM((slot_rows, nz * tok_count), BF16),
            pltpu.VMEM((slot_rows, 128), F32),
            pltpu.VMEM(meta, BF16), pltpu.VMEM((nz, *meta), BF16),
            dma((n, ahead)), dma((n, ahead)), dma((n, max(back, 1))), dma((n, max(back, 1))),
            dma((n, plane)), dma((n, plane)), dma((n,)),
            dma((n,)), dma((n,)), dma((n,)), dma((nz,)), dma((nz,)), dma, dma,
        ]
    )
    vmem = pl.BlockSpec(memory_space=pltpu.VMEM)
    hbm = pl.BlockSpec(memory_space=pl.ANY)
    sizes = ((nx, nz, ny), cap, cap_rows, chunks)
    result = pl.pallas_call(
        functools.partial(kernel, sizes),
        out_shape=jax.ShapeDtypeStruct((half, width), BF16),
        in_specs=[vmem] * 5 + [hbm],
        out_specs=hbm,
        scratch_shapes=scratch,
        compiler_params=pltpu.CompilerParams(
            collective_id=0, has_side_effects=True, vmem_limit_bytes=60 * 1024 * 1024
        ),
    )(grad_out.T, combine.T, routes.T, tasks[None], task_lists, gate_up[0].T)
    parts = 9 if half % 144 == 0 else 1
    return pl.pallas_call(
        hand_over,
        out_shape=jax.ShapeDtypeStruct((half, width), BF16),
        in_specs=[hbm],
        out_specs=hbm,
        scratch_shapes=[pltpu.VMEM((parts, half // parts, width), BF16), dma((parts,)), dma((parts,))],
        compiler_params=pltpu.CompilerParams(vmem_limit_bytes=60 * 1024 * 1024),
    )(result)[None]


def solution(mesh):
    in_specs = (
        P(("exp", "dp"), None),
        P(("exp", "dp"), None),
        P(("exp", "dp"), None),
        P(("exp", "dp")),
        P(),
        P("exp", "dp", None),
    )
    out_specs = P("exp", "dp", None)
    return jax.shard_map(body, mesh=mesh, in_specs=in_specs, out_specs=out_specs, check_vma=False)
```
